256 devices in a mesh: shot: 8 (over x, z_hi), slab: 32 (over z_lo, y, core).
Axes of the slice: x: 4, y: 4, z: 8 (z_hi: 2, z_lo: 4; z = z_hi * 4 + z_lo), core: 2. Of those that a mesh axis runs over, the one named last changes fastest.
Arguments:
- fwd_last: float32 [8, 512, 64, 128], P('shot', 'slab'), may hold values from -6 to 6
- fwd_prev: float32 [8, 512, 64, 128], P('shot', 'slab'), may hold values from -6 to 6
- velocity: float32 [512, 64, 128], P('slab'), may hold values from 0.5 to 1
- aperture: int32 [8, 64, 128], P('shot'), may hold values 0 or 1
- rec_index: int32 [8, 2048], P('shot'), may hold values from 0 to 4194303
- src_index: int32 [8], P('shot'), may hold values from 0 to 4194303
- residual: float32 [8, 32, 2048], P('shot'), may hold values from -6 to 6
Outputs:
- gradient: float32 [512, 64, 128], P('slab', 'shot')
- adjoint_field: float32 [8, 512, 64, 128], P('shot', 'slab')
The draws below stay inside these ranges and needn't reach their ends.
All inputs are finite; a program needn't handle non-finite values. No bound on the sum of `aperture` on one device may be relied on, other than what follows from the above.
Results may differ from the reference program's by a relative error of at most 0.000025.
Values sent between devices are 32-bit elements; how exact they have to be, the bound alone decides.
A program may use at most 256 MiB of HBM per device.

```python
import jax
import jax.numpy as jnp
from jax import lax

NX = 64
NY = 128
STEPS = 32
NREC = 2048
NZ = 512
SHOTS = 8


def with_ends(entries, own_key, least, high):
    longest = entries.shape.index(max(entries.shape))
    spots = []
    for shift in (0, 1):
        where = [jax.random.randint(jax.random.fold_in(own_key, axis), (), 0, length) for axis, length in enumerate(entries.shape)]
        where[longest] = (where[longest] + shift) % entries.shape[longest]
        spots.append(tuple(where))
    return entries.at[spots[0]].set(least).at[spots[1]].set(high)


def shard_levels(rng, dims, split, least, high):
    factor_of, own = 1.0, jax.random.fold_in(rng, 6)
    for dim, parts in split:
        steps = jnp.exp(jax.random.uniform(jax.random.fold_in(own, dim), (parts,), jnp.float32, least / len(split), high / len(split)))
        factor_of = factor_of * jnp.repeat(steps, dims[dim] // parts).reshape([-1 if axis == dim else 1 for axis in range(len(dims))])
    return factor_of


def bell_draw(own_key, shape, width, limit, pieces=(), held_as=jnp.bfloat16):
    gain = shard_levels(own_key, shape, pieces, -0.22, 0.18) if pieces else 1.0
    drawn = jax.random.normal(own_key, shape, jnp.float32) * width * gain
    return jnp.minimum(jnp.maximum(drawn, -limit), limit).astype(held_as)


def setup_inputs(seed: int = 0) -> dict:
    keys = jax.random.split(jax.random.key(seed), 8)
    return {
        "fwd_last": bell_draw(keys[0], (SHOTS, NZ, NX, NY), 1.0, 6.0, ((0, 8), (1, 32)), jnp.float32),
        "fwd_prev": bell_draw(keys[1], (SHOTS, NZ, NX, NY), 1.0, 6.0, ((0, 8), (1, 32)), jnp.float32),
        "velocity": jnp.clip(0.5 + 0.5 * jax.random.uniform(keys[2], (NZ, NX, NY), jnp.float32) ** shard_levels(keys[2], (NZ, NX, NY), ((0, 32),), -0.2, 0.2), 0.5, 1.0),
        "aperture": with_ends((jax.random.randint(keys[3], (SHOTS, NX, NY), 0, 2) < 1).astype(jnp.int32), jax.random.fold_in(keys[3], 1), 0, 1),
        "rec_index": with_ends(jax.random.randint(keys[4], (SHOTS, NREC), 0, NZ * NX * NY), jax.random.fold_in(keys[4], 1), 0, (NZ * NX * NY) - 1).astype(jnp.int32),
        "src_index": with_ends(jax.random.randint(keys[5], (SHOTS,), 0, NZ * NX * NY), jax.random.fold_in(keys[5], 1), 0, (NZ * NX * NY) - 1).astype(jnp.int32),
        "residual": bell_draw(keys[6], (SHOTS, STEPS, NREC), 1.0, 6.0, ((0, 8),), jnp.float32),
    }


COEFS = (-205.0 / 72.0, 8.0 / 5.0, -1.0 / 5.0, 8.0 / 315.0, -1.0 / 560.0)


def second_diff(padded, lower, count):
    centre = padded[:, lower:lower + count]
    total = 3.0 * COEFS[0] * centre
    for k in range(1, 5):
        total = total + COEFS[k] * (padded[:, lower + k:lower + k + count] + padded[:, lower - k:lower - k + count])
    width_x = centre.shape[2]
    width_y = centre.shape[3]
    sides = jnp.pad(centre, ((0, 0), (0, 0), (4, 4), (4, 4)))
    for k in range(1, 5):
        total = total + COEFS[k] * (sides[:, :, 4 + k:4 + k + width_x, 4:4 + width_y] + sides[:, :, 4 - k:4 - k + width_x, 4:4 + width_y])
    for k in range(1, 5):
        total = total + COEFS[k] * (sides[:, :, 4:4 + width_x, 4 + k:4 + k + width_y] + sides[:, :, 4:4 + width_x, 4 - k:4 - k + width_y])
    return total


def ricker(step):
    arg = (jnp.pi * 0.06 * (step - 10.0)) ** 2
    return 10.0 * (1.0 - 2.0 * arg) * jnp.exp(-arg)


def reference(fwd_last, fwd_prev, velocity, aperture, rec_index, src_index, residual):
    coef = (0.4 * velocity) ** 2
    total_cells = NZ * NX * NY

    def laplace(field):
        padded = jnp.pad(field[None], ((0, 0), (4, 4), (0, 0), (0, 0)))
        return second_diff(padded, 4, NZ)[0]

    def one_shot(items):
        u_next, u_cur, gate, receivers, source, trace = items
        gate_f = gate.astype(jnp.float32)[None]
        zero = jnp.zeros((NZ, NX, NY), jnp.float32)

        def advance(k, carry):
            u_next, u_cur, l_next, l_cur, acc = carry
            step = STEPS - 1 - k
            wave = ricker(step.astype(jnp.float32))
            src_field = jnp.zeros((total_cells,), jnp.float32).at[source].add(wave).reshape(NZ, NX, NY)
            rec_field = jnp.zeros((total_cells,), jnp.float32).at[receivers].add(trace[step]).reshape(NZ, NX, NY)
            u_new = 2.0 * u_cur - u_next + coef * (laplace(u_cur) + src_field)
            l_new = 2.0 * l_cur - l_next + coef * (laplace(l_cur) + rec_field)
            acc = acc + gate_f * u_cur * (l_next - 2.0 * l_cur + l_new)
            return (u_cur, u_new, l_cur, l_new, acc)

        out = lax.fori_loop(0, STEPS, advance, (u_next, u_cur, zero, zero, zero))
        return out[4], out[3]

    terms, adjoint_field = lax.map(one_shot, (fwd_last, fwd_prev, aperture, rec_index, src_index, residual))
    gradient = (-2.0 / velocity) * jnp.sum(terms, axis=0)
    return gradient, adjoint_field
```

```python
import functools

import jax
import jax.numpy as jnp
import numpy as np
from jax import lax
from jax.experimental import pallas as pl
from jax.experimental.pallas import tpu as pltpu
from jax.sharding import PartitionSpec as P

SCALE = 5040.0
CENTRE = -43050.0
WEIGHTS = (8064.0, -1008.0, 128.0, -9.0)
HALO = 4
MESH = pl.DeviceIdType.MESH


def ricker(step):
    arg = (jnp.pi * 0.06 * (step - 10.0)) ** 2
    return 10.0 * (1.0 - 2.0 * arg) * jnp.exp(-arg)


def band(size):
    matrix = np.zeros((size, size), np.float32)
    for k, weight in enumerate(WEIGHTS, 1):
        matrix += weight * (np.eye(size, k=k) + np.eye(size, k=-k))
    return matrix


def table_kernel(chunk, rec_ref, res_ref, out_ref, table, picked):
    steps, lanes = res_ref.shape[1], table.shape[1]
    rows = table.shape[0] // steps
    receivers = rec_ref.shape[1]
    cells = rows * lanes
    base = lax.axis_index("slab") * cells
    part = pl.program_id(0)

    @pl.when(part == 0)
    def _():
        group = 8
        rows_each = rows // (receivers // group)

        def scan(i, count):
            for j in range(group):
                r = i * group + j
                local = rec_ref[0, r] - base
                picked[count] = r
                inside = jnp.logical_and(local >= 0, local < cells)
                count = count + inside.astype(jnp.int32)
            clear = pl.multiple_of(i * (rows_each * steps), rows_each * steps)
            table[pl.ds(clear, rows_each * steps)] = jnp.zeros((rows_each * steps, lanes), jnp.float32)
            return count

        count = lax.fori_loop(0, receivers // group, scan, jnp.int32(0))
        lane_ids = lax.broadcasted_iota(jnp.int32, (steps, lanes), 1)

        def add(i, carry):
            r = picked[i]
            local = rec_ref[0, r] - base
            row = local // lanes
            lane = local % lanes
            start = pl.multiple_of((r // lanes) * lanes, lanes)
            traces = res_ref[0, :, pl.ds(start, lanes)]
            moved = pltpu.roll(traces, (lane - r) & (lanes - 1), axis=1)
            place = pl.ds(pl.multiple_of(row * steps, steps), steps)
            table[place] = table[place] + jnp.where(lane_ids == lane, SCALE * moved, 0.0)
            return carry

        lax.fori_loop(0, count, add, 0)

    depth, wide = out_ref.shape[1:3]
    for c in range(chunk):
        n = part * chunk + c

        def layer(z, carry):
            out_ref[c, z] = table[pl.ds(z * wide * steps + n, wide, stride=steps), :]
            return carry

        lax.fori_loop(0, depth, layer, 0, unroll=4)


def receiver_table(rec_index, residual, depth, wide, lanes):
    steps = residual.shape[1]
    chunk = 4
    return pl.pallas_call(
        functools.partial(table_kernel, chunk),
        grid=(steps // chunk,),
        out_shape=jax.ShapeDtypeStruct((steps, depth, wide, lanes), jnp.float32),
        in_specs=[
            pl.BlockSpec(memory_space=pltpu.SMEM),
            pl.BlockSpec(residual.shape, lambda i: (0, 0, 0)),
        ],
        out_specs=pl.BlockSpec((chunk, depth, wide, lanes), lambda i: (i, 0, 0, 0)),
        scratch_shapes=[
            pltpu.VMEM((depth * wide * steps, lanes), jnp.float32),
            pltpu.SMEM((rec_index.shape[1],), jnp.int32),
        ],
        compiler_params=pltpu.CompilerParams(vmem_limit_bytes=32 * 1024 * 1024),
    )(rec_index, residual)


def adjoint_kernel(
    groups, last_ref, prev_ref, vel_ref, gate_ref, src_ref, wave_ref, rec_ref, mx_ref, my_ref,
    grad_ref, adj_ref,
    u_buf, l_buf, coef, src_coef, image, rec_buf, first, second, part_sum,
    u_send, u_recv, l_send, l_recv, rec_sem, io_sem, sum_send, sum_recv,
):
    depth, wide, lanes = last_ref.shape[1:]
    steps = rec_ref.shape[0]
    n_x, n_hi = groups
    shot = lax.axis_index("shot")
    slab = lax.axis_index("slab")
    slabs = lax.axis_size("slab")
    x, hi = shot // n_hi, shot % n_hi
    top = depth + HALO

    load_prev = pltpu.make_async_copy(prev_ref.at[0], u_buf.at[0, pl.ds(HALO, depth)], io_sem.at[0])
    load_last = pltpu.make_async_copy(last_ref.at[0], u_buf.at[1, pl.ds(HALO, depth)], io_sem.at[1])
    load_prev.start()
    load_last.start()

    def load_rec(s):
        slot = lax.rem(s, 2)
        return pltpu.make_async_copy(rec_ref.at[steps - 1 - s], rec_buf.at[slot], rec_sem.at[slot])

    load_rec(0).start()

    empty = jnp.zeros((HALO, wide, lanes), jnp.float32)
    for q in range(2):
        u_buf[q, 0:HALO] = empty
        u_buf[q, top : top + HALO] = empty
        for z in range(0, depth + 2 * HALO, HALO):
            l_buf[q, z : z + HALO] = empty

    barrier = pltpu.get_barrier_semaphore()
    peers = [(lax.rem(x + d, n_x) * n_hi + hi, slab) for d in range(1, n_x)]
    peers += [(x * n_hi + lax.rem(hi + d, n_hi), slab) for d in range(1, n_hi)]
    for peer in peers:
        pl.semaphore_signal(barrier, inc=1, device_id=peer, device_id_type=MESH)

    @pl.when(slab > 0)
    def _():
        pl.semaphore_signal(barrier, inc=1, device_id=(shot, slab - 1), device_id_type=MESH)

    @pl.when(slab < slabs - 1)
    def _():
        pl.semaphore_signal(barrier, inc=1, device_id=(shot, slab + 1), device_id_type=MESH)

    ends = (slab > 0).astype(jnp.int32) + (slab < slabs - 1).astype(jnp.int32)
    pl.semaphore_wait(barrier, len(peers) + ends)

    def down_copy(buf, send, recv, q, source=None):
        return pltpu.make_async_remote_copy(
            src_ref=buf.at[q, pl.ds(HALO, HALO)] if source is None else source,
            dst_ref=buf.at[q, pl.ds(top, HALO)],
            send_sem=send.at[q, 0],
            recv_sem=recv.at[q, 1],
            device_id=(shot, slab - 1),
            device_id_type=MESH,
        )

    def up_copy(buf, send, recv, q, source=None):
        return pltpu.make_async_remote_copy(
            src_ref=buf.at[q, pl.ds(depth, HALO)] if source is None else source,
            dst_ref=buf.at[q, pl.ds(0, HALO)],
            send_sem=send.at[q, 1],
            recv_sem=recv.at[q, 0],
            device_id=(shot, slab + 1),
            device_id_type=MESH,
        )

    @pl.when(slab > 0)
    def _():
        down_copy(u_buf, u_send, u_recv, 0, prev_ref.at[0, pl.ds(0, HALO)]).start()

    @pl.when(slab < slabs - 1)
    def _():
        up_copy(u_buf, u_send, u_recv, 0, prev_ref.at[0, pl.ds(depth - HALO, HALO)]).start()

    ids = lax.broadcasted_iota(jnp.int32, (wide, lanes), 0) * lanes + lax.broadcasted_iota(
        jnp.int32, (wide, lanes), 1
    )
    source = src_ref[0] - slab * (depth * wide * lanes)

    def prepare(z, carry):
        speed = 0.4 * vel_ref[z]
        value = speed * speed
        coef[z] = value * (1.0 / SCALE)
        src_coef[z] = jnp.where(ids == source - z * (wide * lanes), value, 0.0)
        image[:, z] = jnp.zeros((wide // 8, 8, lanes), jnp.float32)
        return carry

    lax.fori_loop(0, depth, prepare, 0)
    load_prev.wait()
    load_last.wait()

    def laplace(buf, q, z):
        f = buf[q, z + HALO]
        hi_part = f.astype(jnp.bfloat16)
        rest = f - hi_part.astype(jnp.float32)
        mid_part = rest.astype(jnp.bfloat16)
        lo_part = (rest - mid_part.astype(jnp.float32)).astype(jnp.bfloat16)
        total = CENTRE * f
        for k, weight in enumerate(WEIGHTS, 1):
            total = total + weight * (buf[q, z + HALO + k] + buf[q, z + HALO - k])
        total = total + jnp.dot(
            mx_ref[...],
            jnp.concatenate([hi_part, mid_part, lo_part], axis=0),
            preferred_element_type=jnp.float32,
        )
        total = total + jnp.dot(
            jnp.concatenate([hi_part, mid_part, lo_part], axis=1),
            my_ref[...],
            preferred_element_type=jnp.float32,
        )
        return f, total

    def u_layers(s, q, first_layer):
        wave = wave_ref[s]
        for z in range(first_layer, first_layer + HALO):
            f, lap = laplace(u_buf, q, z)
            u_buf[1 - q, z + HALO] = (
                2.0 * f - u_buf[1 - q, z + HALO] + coef[z] * lap + wave * src_coef[z]
            )

    def l_layers(s, q, first_layer):
        for z in range(first_layer, first_layer + HALO):
            f, lap = laplace(l_buf, q, z)
            forced = lap + rec_buf[q, z]
            l_buf[1 - q, z + HALO] = 2.0 * f - l_buf[1 - q, z + HALO] + coef[z] * forced
            term = u_buf[q, z + HALO] * forced
            image[:, z] = image[:, z] + term.reshape(wide // 8, 8, lanes)

    has_down, has_up = slab > 0, slab < slabs - 1

    def advance(s, q, buf, send, recv, layers, can_recv, can_wait_send, can_send):
        def both(a, b):
            return a if b is True else jnp.logical_and(a, b)

        for has, copy, edge in ((has_down, down_copy, 0), (has_up, up_copy, 1)):
            @pl.when(both(has, can_recv))
            def _():
                (up_copy if edge == 0 else down_copy)(buf, send, recv, q).wait_recv()

            @pl.when(both(has, can_wait_send))
            def _():
                copy(buf, send, recv, 1 - q).wait_send()

            layers(s, q, 0 if edge == 0 else depth - HALO)

            if can_send is not False:
                @pl.when(both(has, can_send))
                def _():
                    copy(buf, send, recv, 1 - q).start()

        for z in range(HALO, depth - HALO, HALO):
            layers(s, q, z)

    def step(s, carry):
        q = lax.rem(s, 2)
        load_rec(s + 1).start()
        advance(s, q, u_buf, u_send, u_recv, u_layers, True, s >= 1, s < steps - 2)
        load_rec(s).wait()
        advance(s, q, l_buf, l_send, l_recv, l_layers, s >= 1, s >= 2, True)
        return carry

    lax.fori_loop(0, steps - 1, step, 0)
    s_end = steps - 1
    load_rec(s_end).wait()
    advance(s_end, s_end % 2, l_buf, l_send, l_recv, l_layers, True, True, False)

    store = pltpu.make_async_copy(
        l_buf.at[steps % 2, pl.ds(HALO, depth)], adj_ref.at[0], io_sem.at[0]
    )
    store.start()

    for b in range(wide // 8):
        gate = gate_ref[0, 8 * b : 8 * b + 8].astype(jnp.float32)
        image[b] = image[b] * gate

    copies = []
    for d in range(1, n_x):
        target = lax.rem(x + d, n_x)
        copies.append(
            pltpu.make_async_remote_copy(
                src_ref=image.at[pl.ds(target * n_hi, n_hi)],
                dst_ref=first.at[d - 1],
                send_sem=sum_send.at[d - 1],
                recv_sem=sum_recv.at[d - 1],
                device_id=(target * n_hi + hi, slab),
                device_id_type=MESH,
            )
        )
        copies[-1].start()
    for copy in copies:
        copy.wait_recv()
    for h in range(n_hi):
        total = image[x * n_hi + h]
        for d in range(1, n_x):
            total = total + first[d - 1, h]
        part_sum[h] = total
    for d in range(1, n_hi):
        target = lax.rem(hi + d, n_hi)
        copies.append(
            pltpu.make_async_remote_copy(
                src_ref=part_sum.at[target],
                dst_ref=second.at[d - 1],
                send_sem=sum_send.at[n_x - 2 + d],
                recv_sem=sum_recv.at[n_x - 2 + d],
                device_id=(x * n_hi + target, slab),
                device_id_type=MESH,
            )
        )
        copies[-1].start()
        copies[-1].wait_recv()
    total = part_sum[hi]
    for d in range(1, n_hi):
        total = total + second[d - 1]
    speed = vel_ref[:, pl.ds(pl.multiple_of(shot * 8, 8), 8), :]
    grad_ref[...] = (-0.32 / SCALE) * speed * total
    for copy in copies:
        copy.wait_send()
    store.wait()

    for buf, send, recv, q in (
        (u_buf, u_send, u_recv, (steps - 2) % 2),
        (l_buf, l_send, l_recv, (steps - 1) % 2),
    ):
        @pl.when(has_down)
        def _():
            down_copy(buf, send, recv, q).wait_send()

        @pl.when(has_up)
        def _():
            up_copy(buf, send, recv, q).wait_send()


def on_device(groups, fwd_last, fwd_prev, velocity, aperture, rec_index, src_index, residual):
    depth, wide, lanes = fwd_last.shape[1:]
    steps = residual.shape[1]
    n_x, n_hi = groups
    blocks = wide // 8
    table = receiver_table(rec_index, residual, depth, wide, lanes)
    waves = ricker((steps - 1 - jnp.arange(steps, dtype=jnp.int32)).astype(jnp.float32))
    mx = jnp.asarray(np.tile(band(wide), (1, 3)), jnp.bfloat16)
    my = jnp.asarray(np.tile(band(lanes), (3, 1)), jnp.bfloat16)
    hbm = pl.BlockSpec(memory_space=pl.ANY)
    vmem = pl.BlockSpec(memory_space=pltpu.VMEM)
    smem = pl.BlockSpec(memory_space=pltpu.SMEM)
    field = pltpu.VMEM((2, depth + 2 * HALO, wide, lanes), jnp.float32)
    grid = pltpu.VMEM((depth, wide, lanes), jnp.float32)
    pair = pltpu.SemaphoreType.DMA((2, 2))
    return pl.pallas_call(
        functools.partial(adjoint_kernel, groups),
        out_shape=(
            jax.ShapeDtypeStruct((depth, 8, lanes), jnp.float32),
            jax.ShapeDtypeStruct(fwd_last.shape, jnp.float32),
        ),
        in_specs=[hbm, hbm, vmem, vmem, smem, smem, hbm, vmem, vmem],
        out_specs=(vmem, hbm),
        scratch_shapes=[
            field, field, grid, grid,
            pltpu.VMEM((blocks, depth, 8, lanes), jnp.float32),
            pltpu.VMEM((2, depth, wide, lanes), jnp.float32),
            pltpu.VMEM((n_x - 1, n_hi, depth, 8, lanes), jnp.float32),
            pltpu.VMEM((n_hi - 1, depth, 8, lanes), jnp.float32),
            pltpu.VMEM((n_hi, depth, 8, lanes), jnp.float32),
            pair, pair, pair, pair,
            pltpu.SemaphoreType.DMA((2,)),
            pltpu.SemaphoreType.DMA((2,)),
            pltpu.SemaphoreType.DMA((n_x + n_hi - 2,)),
            pltpu.SemaphoreType.DMA((n_x + n_hi - 2,)),
        ],
        compiler_params=pltpu.CompilerParams(
            collective_id=0, has_side_effects=True, vmem_limit_bytes=32 * 1024 * 1024
        ),
    )(fwd_last, fwd_prev, velocity, aperture, src_index, waves, table, mx, my)


def solution(mesh):
    in_specs = (
        P("shot", "slab", None, None),
        P("shot", "slab", None, None),
        P("slab", None, None),
        P("shot", None, None),
        P("shot", None),
        P("shot"),
        P("shot", None, None),
    )
    out_specs = (P("slab", "shot", None), P("shot", "slab", None, None))
    shots = mesh.shape["shot"]
    groups = (shots // 2, 2)
    return jax.shard_map(
        functools.partial(on_device, groups),
        mesh=mesh, in_specs=in_specs, out_specs=out_specs, check_vma=False,
    )
```

```python
import functools

import jax
import jax.numpy as jnp
import numpy as np
from jax import lax
from jax.experimental import pallas as pl
from jax.experimental.pallas import tpu as pltpu
from jax.sharding import PartitionSpec as P

SCALE = 5040.0
CENTRE = -43050.0
WEIGHTS = (8064.0, -1008.0, 128.0, -9.0)
HALO = 4
MESH = pl.DeviceIdType.MESH


def ricker(step):
    arg = (jnp.pi * 0.06 * (step - 10.0)) ** 2
    return 10.0 * (1.0 - 2.0 * arg) * jnp.exp(-arg)


def band(size):
    matrix = np.zeros((size, size), np.float32)
    for k, weight in enumerate(WEIGHTS, 1):
        matrix += weight * (np.eye(size, k=k) + np.eye(size, k=-k))
    return matrix


def table_kernel(first_row, rec_ref, res_ref, table, picked):
    steps, receivers = res_ref.shape[1:]
    lanes = table.shape[1]
    rows = table.shape[0] // steps
    cells = rows * lanes
    base = (lax.axis_index("slab") * (rows - 2 * first_row) - first_row) * lanes
    group = 8
    clear_rows = rows * steps // (receivers // group)

    def scan(i, count):
        for j in range(group):
            r = i * group + j
            local = rec_ref[0, r] - base
            picked[count] = r
            inside = jnp.logical_and(local >= 0, local < cells)
            count = count + inside.astype(jnp.int32)
        clear = pl.multiple_of(i * clear_rows, clear_rows)
        table[pl.ds(clear, clear_rows)] = jnp.zeros((clear_rows, lanes), jnp.float32)
        return count

    count = lax.fori_loop(0, receivers // group, scan, jnp.int32(0))
    lane_ids = lax.broadcasted_iota(jnp.int32, (steps, lanes), 1)
    together = 4

    def add(i, carry):
        todo = []
        for j in range(together):
            index = i * together + j
            r = picked[jnp.minimum(index, count - 1)]
            local = rec_ref[0, r] - base
            row = local // lanes
            lane = local % lanes
            start = pl.multiple_of((r // lanes) * lanes, lanes)
            traces = res_ref[0, :, pl.ds(start, lanes)]
            moved = pltpu.roll(traces, (lane - r) & (lanes - 1), axis=1)
            chosen = jnp.where(index < count, lane, -1)
            todo.append((row, jnp.where(lane_ids == chosen, SCALE * moved, 0.0)))
        for row, value in todo:
            for n in range(0, steps, 8):
                place = pl.ds(row + n * rows, 8, stride=rows)
                table[place, :] = table[place, :] + value[n : n + 8]
        return carry

    lax.fori_loop(0, (count + together - 1) // together, add, 0)


def receiver_table(rec_index, residual, depth, wide, lanes):
    steps = residual.shape[1]
    vmem = pl.BlockSpec(memory_space=pltpu.VMEM)
    rows = (depth + 2 * HALO) * wide
    return pl.pallas_call(
        functools.partial(table_kernel, HALO * wide),
        out_shape=jax.ShapeDtypeStruct((steps * rows, lanes), jnp.float32),
        in_specs=[pl.BlockSpec(memory_space=pltpu.SMEM), vmem],
        out_specs=vmem,
        scratch_shapes=[pltpu.SMEM((rec_index.shape[1],), jnp.int32)],
        compiler_params=pltpu.CompilerParams(vmem_limit_bytes=4 * 1024 * 1024),
    )(rec_index, residual)


def adjoint_kernel(
    groups, last_ref, prev_ref, vel_ref, gate_ref, src_ref, wave_ref, rec_ref, mx_ref, my_ref,
    grad_ref, adj_ref,
    u_even, l_even, u_odd, l_odd, coef, src_coef, vel_halo, image, first, second, part_sum,
    u_send, u_recv, l_send, l_recv, io_sem, start_send, start_recv, sum_send, sum_recv,
):
    depth, wide, lanes = last_ref.shape[1:]
    ring = 2 * HALO
    blocks = wave_ref.shape[0] // 2
    steps = 2 * blocks
    ext_rows = (depth + 2 * HALO) * wide
    n_x, n_hi = groups
    shot = lax.axis_index("shot")
    slab = lax.axis_index("slab")
    slabs = lax.axis_size("slab")
    x, hi = shot // n_hi, shot % n_hi
    has_down, has_up = slab > 0, slab < slabs - 1

    load_prev = pltpu.make_async_copy(prev_ref.at[0], u_even.at[0, pl.ds(ring, depth)], io_sem.at[0])
    load_last = pltpu.make_async_copy(last_ref.at[0], u_odd.at[pl.ds(HALO, depth)], io_sem.at[1])
    load_prev.start()
    load_last.start()

    empty = jnp.zeros((HALO, wide, lanes), jnp.float32)
    for z in range(0, depth + 2 * ring, HALO):
        l_even[0, z : z + HALO] = empty
        l_even[1, z : z + HALO] = empty
    for z in (0, HALO, depth + ring, depth + ring + HALO):
        u_even[0, z : z + HALO] = empty
        u_even[1, z : z + HALO] = empty
    for z in range(0, depth + 2 * HALO, HALO):
        l_odd[z : z + HALO] = empty
    for side, z in ((0, 0), (1, depth + HALO)):
        u_odd[z : z + HALO] = empty
        vel_halo[side] = empty

    barrier = pltpu.get_barrier_semaphore()
    peers = [(lax.rem(x + d, n_x) * n_hi + hi, slab) for d in range(1, n_x)]
    peers += [(x * n_hi + lax.rem(hi + d, n_hi), slab) for d in range(1, n_hi)]
    for peer in peers:
        pl.semaphore_signal(barrier, inc=1, device_id=peer, device_id_type=MESH)

    @pl.when(has_down)
    def _():
        pl.semaphore_signal(barrier, inc=1, device_id=(shot, slab - 1), device_id_type=MESH)

    @pl.when(has_up)
    def _():
        pl.semaphore_signal(barrier, inc=1, device_id=(shot, slab + 1), device_id_type=MESH)

    pl.semaphore_wait(barrier, len(peers) + has_down.astype(jnp.int32) + has_up.astype(jnp.int32))

    def remote(src, dst, send, recv, target):
        return pltpu.make_async_remote_copy(
            src_ref=src, dst_ref=dst, send_sem=send, recv_sem=recv,
            device_id=target, device_id_type=MESH,
        )

    def halo_copy(buf, send, recv, q, side, source=None):
        if side == 0:
            src, dst = buf.at[q, pl.ds(ring, ring)], buf.at[q, pl.ds(depth + ring, ring)]
        else:
            src, dst = buf.at[q, pl.ds(depth, ring)], buf.at[q, pl.ds(0, ring)]
        return remote(
            src if source is None else source, dst, send.at[q, side], recv.at[q, 1 - side],
            (shot, slab + (1 if side else -1)),
        )

    def start_copies(side):
        near = pl.ds(depth - HALO, HALO) if side else pl.ds(0, HALO)
        wider = pl.ds(depth - ring, ring) if side else pl.ds(0, ring)
        odd_place = pl.ds(0, HALO) if side else pl.ds(depth + HALO, HALO)
        target = (shot, slab + (1 if side else -1))
        return (
            remote(
                vel_ref.at[near], vel_halo.at[1 - side],
                start_send.at[0, side], start_recv.at[0, 1 - side], target,
            ),
            halo_copy(u_even, u_send, u_recv, 0, side, prev_ref.at[0, wider]),
            remote(
                last_ref.at[0, near], u_odd.at[odd_place],
                start_send.at[1, side], start_recv.at[1, 1 - side], target,
            ),
        )

    sides = ((0, has_down), (1, has_up))
    for side, has in sides:
        @pl.when(has)
        def _():
            for copy in start_copies(side):
                copy.start()

    ids = lax.broadcasted_iota(jnp.int32, (wide, lanes), 0) * lanes + lax.broadcasted_iota(
        jnp.int32, (wide, lanes), 1
    )
    source = src_ref[0] - slab * (depth * wide * lanes)

    def prepare(z, speed):
        speed = 0.4 * speed
        value = speed * speed
        coef[z + HALO] = value * (1.0 / SCALE)
        src_coef[z + HALO] = jnp.where(ids == source - z * (wide * lanes), value, 0.0)

    def prepare_own(z, carry):
        prepare(z, vel_ref[z])
        image[:, z] = jnp.zeros((wide // 8, 8, lanes), jnp.float32)
        return carry

    lax.fori_loop(0, depth, prepare_own, 0)
    load_prev.wait()
    load_last.wait()
    for side, has in sides:
        @pl.when(has)
        def _():
            velocity_in, _, last_in = start_copies(1 - side)
            velocity_in.wait_recv()
            last_in.wait_recv()

        for z in range(HALO):
            prepare(z + (depth if side else -HALO), vel_halo[side, z])

    def laplace(read, z):
        f = read(z)
        hi_part = f.astype(jnp.bfloat16)
        rest = f - hi_part.astype(jnp.float32)
        mid_part = rest.astype(jnp.bfloat16)
        lo_part = (rest - mid_part.astype(jnp.float32)).astype(jnp.bfloat16)
        total = CENTRE * f
        for k, weight in enumerate(WEIGHTS, 1):
            total = total + weight * (read(z + k) + read(z - k))
        total = total + jnp.dot(
            mx_ref[...],
            jnp.concatenate([hi_part, mid_part, lo_part], axis=0),
            preferred_element_type=jnp.float32,
        )
        total = total + jnp.dot(
            jnp.concatenate([hi_part, mid_part, lo_part], axis=1),
            my_ref[...],
            preferred_element_type=jnp.float32,
        )
        return f, total

    def update(even, odd, q, to_odd, is_l, wave, rec_start, layers):
        read_even = lambda z: even[q, z + ring]
        read_odd = lambda z: odd[z + HALO]
        for z in layers:
            f, lap = laplace(read_even if to_odd else read_odd, z)
            earlier = (read_odd if to_odd else read_even)(z)
            place = z + HALO
            if is_l:
                start = pl.multiple_of(rec_start + place * wide, 8)
                lap = lap + rec_ref[pl.ds(start, wide), :]
                if 0 <= z < depth:
                    now = u_even[q, z + ring] if to_odd else u_odd[place]
                    image[:, z] = image[:, z] + (now * lap).reshape(wide // 8, 8, lanes)
                fresh = 2.0 * f - earlier + coef[place] * lap
            else:
                fresh = 2.0 * f - earlier + coef[place] * lap + wave * src_coef[place]
            if to_odd:
                odd[place] = fresh
            else:
                even[1 - q, z + ring] = fresh

    def advance(b, q, even, odd, send, recv, is_l):
        waves = (wave_ref[2 * b], wave_ref[2 * b + 1])
        rec_starts = [(steps - 1 - (2 * b + i)) * ext_rows for i in range(2)]

        def layers(to_odd, some):
            i = 0 if to_odd else 1
            update(even, odd, q, to_odd, is_l, waves[i], rec_starts[i], some)

        more = b < blocks - 1
        can_recv = b >= 1 if is_l else b >= 0
        can_wait_send = b >= 2 if is_l else jnp.logical_and(b >= 1, more)
        half = depth // 2
        layers(True, range(HALO, depth - HALO))
        for side, has in sides:
            @pl.when(jnp.logical_and(has, can_recv))
            def _():
                halo_copy(even, send, recv, q, 1 - side).wait_recv()

            @pl.when(jnp.logical_and(has, can_wait_send))
            def _():
                halo_copy(even, send, recv, 1 - q, side).wait_send()

            first_half = side == 0
            layers(True, range(-HALO, HALO) if first_half else range(depth - HALO, depth + HALO))
            second_step = range(half) if first_half else range(half, depth)
            if is_l:
                layers(False, second_step)
            else:
                @pl.when(more)
                def _():
                    layers(False, second_step)

            @pl.when(jnp.logical_and(has, more))
            def _():
                halo_copy(even, send, recv, 1 - q, side).start()

    def block(b, carry):
        q = lax.rem(b, 2)
        advance(b, q, u_even, u_odd, u_send, u_recv, False)
        advance(b, q, l_even, l_odd, l_send, l_recv, True)
        return carry

    lax.fori_loop(0, blocks, block, 0)
    store = pltpu.make_async_copy(
        l_even.at[blocks % 2, pl.ds(ring, depth)], adj_ref.at[0], io_sem.at[0]
    )
    store.start()

    parts = 2
    rows = depth // parts

    def spread(c, d):
        target = lax.rem(x + d, n_x)
        return remote(
            image.at[pl.ds(target * n_hi, n_hi), pl.ds(c * rows, rows)], first.at[c, d - 1],
            sum_send.at[c, d - 1], sum_recv.at[c, d - 1], (target * n_hi + hi, slab),
        )

    def gather(c, d):
        target = lax.rem(hi + d, n_hi)
        return remote(
            part_sum.at[c, target], second.at[c, d - 1],
            sum_send.at[c, n_x - 2 + d], sum_recv.at[c, n_x - 2 + d], (x * n_hi + target, slab),
        )

    for c in range(parts):
        for p in range(wide // 8):
            gate = gate_ref[0, 8 * p : 8 * p + 8].astype(jnp.float32)
            image[p, c * rows : (c + 1) * rows] = image[p, c * rows : (c + 1) * rows] * gate
        for d in range(1, n_x):
            spread(c, d).start()
    for c in range(parts):
        for d in range(1, n_x):
            spread(c, d).wait_recv()
        for h in range(n_hi):
            total = image[x * n_hi + h, c * rows : (c + 1) * rows]
            for d in range(1, n_x):
                total = total + first[c, d - 1, h]
            part_sum[c, h] = total
        for d in range(1, n_hi):
            gather(c, d).start()
    for c in range(parts):
        for d in range(1, n_hi):
            gather(c, d).wait_recv()
        total = part_sum[c, hi]
        for d in range(1, n_hi):
            total = total + second[c, d - 1]
        speed = vel_ref[pl.ds(c * rows, rows), pl.ds(pl.multiple_of(shot * 8, 8), 8), :]
        grad_ref[pl.ds(c * rows, rows)] = (-0.32 / SCALE) * speed * total
    for c in range(parts):
        for d in range(1, n_x):
            spread(c, d).wait_send()
        for d in range(1, n_hi):
            gather(c, d).wait_send()
    store.wait()

    for side, has in sides:
        @pl.when(has)
        def _():
            velocity_out, _, last_out = start_copies(side)
            velocity_out.wait_send()
            last_out.wait_send()
            halo_copy(u_even, u_send, u_recv, blocks % 2, side).wait_send()
            halo_copy(u_even, u_send, u_recv, (blocks - 1) % 2, side).wait_send()
            halo_copy(l_even, l_send, l_recv, (blocks - 1) % 2, side).wait_send()


def on_device(groups, fwd_last, fwd_prev, velocity, aperture, rec_index, src_index, residual):
    depth, wide, lanes = fwd_last.shape[1:]
    steps = residual.shape[1]
    n_x, n_hi = groups
    table = receiver_table(rec_index, residual, depth, wide, lanes)
    waves = ricker((steps - 1 - jnp.arange(steps, dtype=jnp.int32)).astype(jnp.float32))
    mx = jnp.asarray(np.tile(band(wide), (1, 3)), jnp.bfloat16)
    my = jnp.asarray(np.tile(band(lanes), (3, 1)), jnp.bfloat16)
    hbm = pl.BlockSpec(memory_space=pl.ANY)
    vmem = pl.BlockSpec(memory_space=pltpu.VMEM)
    smem = pl.BlockSpec(memory_space=pltpu.SMEM)
    even = pltpu.VMEM((2, depth + 4 * HALO, wide, lanes), jnp.float32)
    odd = pltpu.VMEM((depth + 2 * HALO, wide, lanes), jnp.float32)
    pair = pltpu.SemaphoreType.DMA((2, 2))
    parts = 2
    return pl.pallas_call(
        functools.partial(adjoint_kernel, groups),
        out_shape=(
            jax.ShapeDtypeStruct((depth, 8, lanes), jnp.float32),
            jax.ShapeDtypeStruct(fwd_last.shape, jnp.float32),
        ),
        in_specs=[hbm, hbm, vmem, vmem, smem, smem, vmem, vmem, vmem],
        out_specs=(vmem, hbm),
        scratch_shapes=[
            even, even, odd, odd, odd, odd,
            pltpu.VMEM((2, HALO, wide, lanes), jnp.float32),
            pltpu.VMEM((wide // 8, depth, 8, lanes), jnp.float32),
            pltpu.VMEM((parts, n_x - 1, n_hi, depth // parts, 8, lanes), jnp.float32),
            pltpu.VMEM((parts, n_hi - 1, depth // parts, 8, lanes), jnp.float32),
            pltpu.VMEM((parts, n_hi, depth // parts, 8, lanes), jnp.float32),
            pair, pair, pair, pair,
            pltpu.SemaphoreType.DMA((2,)),
            pair, pair,
            pltpu.SemaphoreType.DMA((parts, n_x + n_hi - 2)),
            pltpu.SemaphoreType.DMA((parts, n_x + n_hi - 2)),
        ],
        compiler_params=pltpu.CompilerParams(
            collective_id=0, has_side_effects=True, vmem_limit_bytes=16 * 1024 * 1024
        ),
    )(fwd_last, fwd_prev, velocity, aperture, src_index, waves, table, mx, my)


def solution(mesh):
    in_specs = (
        P("shot", "slab", None, None),
        P("shot", "slab", None, None),
        P("slab", None, None),
        P("shot", None, None),
        P("shot", None),
        P("shot"),
        P("shot", None, None),
    )
    out_specs = (P("slab", "shot", None), P("shot", "slab", None, None))
    shots = mesh.shape["shot"]
    groups = (shots // 2, 2)
    return jax.shard_map(
        functools.partial(on_device, groups),
        mesh=mesh, in_specs=in_specs, out_specs=out_specs, check_vma=False,
    )
```

```python
import functools

import jax
import jax.numpy as jnp
import numpy as np
from jax import lax
from jax.experimental import pallas as pl
from jax.experimental.pallas import tpu as pltpu
from jax.sharding import PartitionSpec as P

SCALE = 5040.0
CENTRE = -43050.0
WEIGHTS = (8064.0, -1008.0, 128.0, -9.0)
HALO = 4
MESH = pl.DeviceIdType.MESH


def ricker(step):
    arg = (jnp.pi * 0.06 * (step - 10.0)) ** 2
    return 10.0 * (1.0 - 2.0 * arg) * jnp.exp(-arg)


def band(size):
    matrix = np.zeros((size, size), np.float32)
    for k, weight in enumerate(WEIGHTS, 1):
        matrix += weight * (np.eye(size, k=k) + np.eye(size, k=-k))
    return matrix


def table_kernel(first_row, rec_ref, res_ref, table, picked):
    steps, receivers = res_ref.shape[1:]
    lanes = table.shape[1]
    rows = table.shape[0] // steps
    cells = rows * lanes
    base = (lax.axis_index("slab") * (rows - 2 * first_row) - first_row) * lanes
    group = 8
    clear_rows = rows * steps // (receivers // group)

    def scan(i, count):
        for j in range(group):
            r = i * group + j
            local = rec_ref[0, r] - base
            picked[count] = r
            inside = jnp.logical_and(local >= 0, local < cells)
            count = count + inside.astype(jnp.int32)
        clear = pl.multiple_of(i * clear_rows, clear_rows)
        table[pl.ds(clear, clear_rows)] = jnp.zeros((clear_rows, lanes), jnp.float32)
        return count

    count = lax.fori_loop(0, receivers // group, scan, jnp.int32(0))
    lane_ids = lax.broadcasted_iota(jnp.int32, (steps, lanes), 1)
    together = 4

    def add(i, carry):
        todo = []
        for j in range(together):
            index = i * together + j
            r = picked[jnp.minimum(index, count - 1)]
            local = rec_ref[0, r] - base
            row = local // lanes
            lane = local % lanes
            start = pl.multiple_of((r // lanes) * lanes, lanes)
            traces = res_ref[0, :, pl.ds(start, lanes)]
            moved = pltpu.roll(traces, (lane - r) & (lanes - 1), axis=1)
            chosen = jnp.where(index < count, lane, -1)
            todo.append((row, jnp.where(lane_ids == chosen, SCALE * moved, 0.0)))
        for row, value in todo:
            places = [pl.ds(row + n * rows, 8, stride=rows) for n in range(0, steps, 8)]
            held = [table[place, :] for place in places]
            for n, place in enumerate(places):
                table[place, :] = held[n] + value[8 * n : 8 * n + 8]
        return carry

    lax.fori_loop(0, (count + together - 1) // together, add, 0)


def receiver_table(rec_index, residual, depth, wide, lanes):
    steps = residual.shape[1]
    vmem = pl.BlockSpec(memory_space=pltpu.VMEM)
    rows = (depth + 2 * HALO) * wide
    return pl.pallas_call(
        functools.partial(table_kernel, HALO * wide),
        out_shape=jax.ShapeDtypeStruct((steps * rows, lanes), jnp.float32),
        in_specs=[pl.BlockSpec(memory_space=pltpu.SMEM), vmem],
        out_specs=vmem,
        scratch_shapes=[pltpu.SMEM((rec_index.shape[1],), jnp.int32)],
        compiler_params=pltpu.CompilerParams(vmem_limit_bytes=4 * 1024 * 1024),
    )(rec_index, residual)


def adjoint_kernel(
    groups, last_ref, prev_ref, vel_ref, gate_ref, src_ref, wave_ref, rec_ref, mx_ref, my_ref,
    grad_ref, adj_ref,
    u_even, l_even, u_odd, l_odd, coef, src_coef, vel_halo, image, first, second, part_sum,
    u_send, u_recv, l_send, l_recv, io_sem, start_send, start_recv, sum_send, sum_recv,
):
    depth, wide, lanes = last_ref.shape[1:]
    ring = 2 * HALO
    blocks = wave_ref.shape[0] // 2
    steps = 2 * blocks
    ext_rows = (depth + 2 * HALO) * wide
    n_x, n_hi = groups
    shot = lax.axis_index("shot")
    slab = lax.axis_index("slab")
    slabs = lax.axis_size("slab")
    x, hi = shot // n_hi, shot % n_hi
    has_down, has_up = slab > 0, slab < slabs - 1

    load_prev = pltpu.make_async_copy(prev_ref.at[0], u_even.at[0, pl.ds(ring, depth)], io_sem.at[0])
    load_last = pltpu.make_async_copy(last_ref.at[0], u_odd.at[pl.ds(HALO, depth)], io_sem.at[1])
    load_prev.start()
    load_last.start()

    empty = jnp.zeros((HALO, wide, lanes), jnp.float32)
    for z in range(0, depth + 2 * ring, HALO):
        l_even[0, z : z + HALO] = empty
        l_even[1, z : z + HALO] = empty
    for z in (0, HALO, depth + ring, depth + ring + HALO):
        u_even[0, z : z + HALO] = empty
        u_even[1, z : z + HALO] = empty
    for z in range(0, depth + 2 * HALO, HALO):
        l_odd[z : z + HALO] = empty
    for side, z in ((0, 0), (1, depth + HALO)):
        u_odd[z : z + HALO] = empty
        vel_halo[side] = empty

    barrier = pltpu.get_barrier_semaphore()
    peers = [(lax.rem(x + d, n_x) * n_hi + hi, slab) for d in range(1, n_x)]
    peers += [(x * n_hi + lax.rem(hi + d, n_hi), slab) for d in range(1, n_hi)]
    for peer in peers:
        pl.semaphore_signal(barrier, inc=1, device_id=peer, device_id_type=MESH)

    @pl.when(has_down)
    def _():
        pl.semaphore_signal(barrier, inc=1, device_id=(shot, slab - 1), device_id_type=MESH)

    @pl.when(has_up)
    def _():
        pl.semaphore_signal(barrier, inc=1, device_id=(shot, slab + 1), device_id_type=MESH)

    pl.semaphore_wait(barrier, len(peers) + has_down.astype(jnp.int32) + has_up.astype(jnp.int32))

    def remote(src, dst, send, recv, target):
        return pltpu.make_async_remote_copy(
            src_ref=src, dst_ref=dst, send_sem=send, recv_sem=recv,
            device_id=target, device_id_type=MESH,
        )

    def halo_layers(side, half):
        return depth - HALO * (half + 1) if side else HALO * half

    def halo_copy(buf, send, recv, q, side, half, source=None):
        start = halo_layers(side, half)
        place = start - depth if side else start + depth
        src = buf.at[q, pl.ds(ring + start, HALO)] if source is None else source
        return remote(
            src, buf.at[q, pl.ds(ring + place, HALO)],
            send.at[q, side, half], recv.at[q, 1 - side, half], (shot, slab + (1 if side else -1)),
        )

    def start_copies(side):
        near = pl.ds(halo_layers(side, 0), HALO)
        far = pl.ds(halo_layers(side, 1), HALO)
        odd_place = pl.ds(0, HALO) if side else pl.ds(depth + HALO, HALO)
        target = (shot, slab + (1 if side else -1))
        return (
            remote(
                vel_ref.at[near], vel_halo.at[1 - side],
                start_send.at[0, side], start_recv.at[0, 1 - side], target,
            ),
            halo_copy(u_even, u_send, u_recv, 0, side, 0, prev_ref.at[0, near]),
            halo_copy(u_even, u_send, u_recv, 0, side, 1, prev_ref.at[0, far]),
            remote(
                last_ref.at[0, near], u_odd.at[odd_place],
                start_send.at[1, side], start_recv.at[1, 1 - side], target,
            ),
        )

    sides = ((0, has_down), (1, has_up))
    for side, has in sides:
        @pl.when(has)
        def _():
            for copy in start_copies(side):
                copy.start()

    ids = lax.broadcasted_iota(jnp.int32, (wide, lanes), 0) * lanes + lax.broadcasted_iota(
        jnp.int32, (wide, lanes), 1
    )
    source = src_ref[0] - slab * (depth * wide * lanes)

    def prepare(z, speed):
        speed = 0.4 * speed
        value = speed * speed
        coef[z + HALO] = value * (1.0 / SCALE)
        src_coef[z + HALO] = jnp.where(ids == source - z * (wide * lanes), value, 0.0)

    def prepare_own(z, carry):
        prepare(z, vel_ref[z])
        image[:, z] = jnp.zeros((wide // 8, 8, lanes), jnp.float32)
        return carry

    lax.fori_loop(0, depth, prepare_own, 0)
    load_prev.wait()
    load_last.wait()
    for side, has in sides:
        @pl.when(has)
        def _():
            velocity_in, _, _, last_in = start_copies(1 - side)
            velocity_in.wait_recv()
            last_in.wait_recv()

        for z in range(HALO):
            prepare(z + (depth if side else -HALO), vel_halo[side, z])

    def laplace(read, z):
        f = read(z)
        hi_part = f.astype(jnp.bfloat16)
        rest = f - hi_part.astype(jnp.float32)
        mid_part = rest.astype(jnp.bfloat16)
        lo_part = (rest - mid_part.astype(jnp.float32)).astype(jnp.bfloat16)
        total = CENTRE * f
        for k, weight in enumerate(WEIGHTS, 1):
            total = total + weight * (read(z + k) + read(z - k))
        total = total + jnp.dot(
            mx_ref[...],
            jnp.concatenate([hi_part, mid_part, lo_part], axis=0),
            preferred_element_type=jnp.float32,
        )
        total = total + jnp.dot(
            jnp.concatenate([hi_part, mid_part, lo_part], axis=1),
            my_ref[...],
            preferred_element_type=jnp.float32,
        )
        return f, total

    def update(even, odd, q, to_odd, is_l, wave, rec_start, layers):
        read_even = lambda z: even[q, z + ring]
        read_odd = lambda z: odd[z + HALO]
        for z in layers:
            f, lap = laplace(read_even if to_odd else read_odd, z)
            earlier = (read_odd if to_odd else read_even)(z)
            place = z + HALO
            if is_l:
                start = pl.multiple_of(rec_start + place * wide, 8)
                lap = lap + rec_ref[pl.ds(start, wide), :]
                if 0 <= z < depth:
                    now = u_even[q, z + ring] if to_odd else u_odd[place]
                    image[:, z] = image[:, z] + (now * lap).reshape(wide // 8, 8, lanes)
                fresh = 2.0 * f - earlier + coef[place] * lap
            else:
                fresh = 2.0 * f - earlier + coef[place] * lap + wave * src_coef[place]
            if to_odd:
                odd[place] = fresh
            else:
                even[1 - q, z + ring] = fresh

    assert depth == 4 * HALO
    fields = (
        (u_even, u_odd, u_send, u_recv, False),
        (l_even, l_odd, l_send, l_recv, True),
    )

    def layers(b, q, field, to_odd, some):
        even, odd, _, _, is_l = field
        i = 0 if to_odd else 1
        step = 2 * b + i
        rec_start = (steps - 1 - step) * ext_rows
        update(even, odd, q, to_odd, is_l, wave_ref[step], rec_start, some)

    def inner(b, q, field):
        layers(b, q, field, True, range(HALO, depth - HALO))

    def when(cond, run):
        if cond is True:
            run()
        else:
            pl.when(cond)(run)

    def both(a, b):
        return a if b is True else jnp.logical_and(a, b)

    def arrive(q, field, side, half, some):
        even, _, send, recv, _ = field
        when(both(sides[side][1], some), halo_copy(even, send, recv, q, 1 - side, half).wait_recv)

    def depart(b, q, field, side, half, sent_before, more):
        even, _, send, recv, _ = field
        has = sides[side][1]
        start = halo_layers(side, half)

        def second():
            when(both(has, sent_before), halo_copy(even, send, recv, 1 - q, side, half).wait_send)
            layers(b, q, field, False, range(start, start + HALO))

        if field[4]:
            second()
        else:
            when(more, second)
        when(both(has, more), halo_copy(even, send, recv, 1 - q, side, half).start)

    near_layers = (range(HALO), range(depth - HALO, depth))
    far_layers = (range(-HALO, 0), range(depth, depth + HALO))

    def near_first(i, field, side, half):
        b, q = 2 * i, 0
        arrive(q, field, side, half, i >= 1 if field[4] else True)
        layers(b, q, field, True, far_layers[side] if half else near_layers[side])
        depart(b, q, field, side, 1 - half, i >= 1, True)

    def far_first(i, field, side):
        b, q = 2 * i + 1, 1
        more = b < blocks - 1
        arrive(q, field, side, 1, True)
        arrive(q, field, side, 0, True)
        layers(b, q, field, True, near_layers[side])
        layers(b, q, field, True, far_layers[side])
        for half in range(2):
            depart(b, q, field, side, half, i >= 1 if field[4] else True, more)

    def two_blocks(i, carry):
        u, l = fields
        inner(2 * i, 0, u)
        near_first(i, u, 0, 0)
        near_first(i, u, 1, 0)
        inner(2 * i, 0, l)
        near_first(i, u, 0, 1)
        near_first(i, u, 1, 1)
        near_first(i, l, 0, 0)
        near_first(i, l, 1, 0)
        inner(2 * i + 1, 1, u)
        near_first(i, l, 0, 1)
        near_first(i, l, 1, 1)
        far_first(i, u, 0)
        far_first(i, u, 1)
        inner(2 * i + 1, 1, l)
        far_first(i, l, 0)
        far_first(i, l, 1)
        return carry

    lax.fori_loop(0, blocks // 2, two_blocks, 0)
    store = pltpu.make_async_copy(
        l_even.at[blocks % 2, pl.ds(ring, depth)], adj_ref.at[0], io_sem.at[0]
    )
    store.start()

    parts = 2
    rows = depth // parts

    def spread(c, d):
        target = lax.rem(x + d, n_x)
        return remote(
            image.at[pl.ds(target * n_hi, n_hi), pl.ds(c * rows, rows)], first.at[c, d - 1],
            sum_send.at[c, d - 1], sum_recv.at[c, d - 1], (target * n_hi + hi, slab),
        )

    def gather(c, d):
        target = lax.rem(hi + d, n_hi)
        return remote(
            part_sum.at[c, target], second.at[c, d - 1],
            sum_send.at[c, n_x - 2 + d], sum_recv.at[c, n_x - 2 + d], (x * n_hi + target, slab),
        )

    for c in range(parts):
        for p in range(wide // 8):
            gate = gate_ref[0, 8 * p : 8 * p + 8].astype(jnp.float32)
            image[p, c * rows : (c + 1) * rows] = image[p, c * rows : (c + 1) * rows] * gate
        for d in range(1, n_x):
            spread(c, d).start()
    for c in range(parts):
        for d in range(1, n_x):
            spread(c, d).wait_recv()
        for h in range(n_hi):
            total = image[x * n_hi + h, c * rows : (c + 1) * rows]
            for d in range(1, n_x):
                total = total + first[c, d - 1, h]
            part_sum[c, h] = total
        for d in range(1, n_hi):
            gather(c, d).start()
    for c in range(parts):
        for d in range(1, n_hi):
            gather(c, d).wait_recv()
        total = part_sum[c, hi]
        for d in range(1, n_hi):
            total = total + second[c, d - 1]
        speed = vel_ref[pl.ds(c * rows, rows), pl.ds(pl.multiple_of(shot * 8, 8), 8), :]
        grad_ref[pl.ds(c * rows, rows)] = (-0.32 / SCALE) * speed * total
    for c in range(parts):
        for d in range(1, n_x):
            spread(c, d).wait_send()
        for d in range(1, n_hi):
            gather(c, d).wait_send()
    store.wait()

    for side, has in sides:
        @pl.when(has)
        def _():
            velocity_out, _, _, last_out = start_copies(side)
            velocity_out.wait_send()
            last_out.wait_send()
            for half in range(2):
                halo_copy(u_even, u_send, u_recv, 0, side, half).wait_send()
                halo_copy(u_even, u_send, u_recv, 1, side, half).wait_send()
                halo_copy(l_even, l_send, l_recv, 1, side, half).wait_send()


def on_device(groups, fwd_last, fwd_prev, velocity, aperture, rec_index, src_index, residual):
    depth, wide, lanes = fwd_last.shape[1:]
    steps = residual.shape[1]
    n_x, n_hi = groups
    table = receiver_table(rec_index, residual, depth, wide, lanes)
    waves = ricker((steps - 1 - jnp.arange(steps, dtype=jnp.int32)).astype(jnp.float32))
    mx = jnp.asarray(np.tile(band(wide), (1, 3)), jnp.bfloat16)
    my = jnp.asarray(np.tile(band(lanes), (3, 1)), jnp.bfloat16)
    hbm = pl.BlockSpec(memory_space=pl.ANY)
    vmem = pl.BlockSpec(memory_space=pltpu.VMEM)
    smem = pl.BlockSpec(memory_space=pltpu.SMEM)
    even = pltpu.VMEM((2, depth + 4 * HALO, wide, lanes), jnp.float32)
    odd = pltpu.VMEM((depth + 2 * HALO, wide, lanes), jnp.float32)
    pair = pltpu.SemaphoreType.DMA((2, 2))
    triple = pltpu.SemaphoreType.DMA((2, 2, 2))
    parts = 2
    return pl.pallas_call(
        functools.partial(adjoint_kernel, groups),
        out_shape=(
            jax.ShapeDtypeStruct((depth, 8, lanes), jnp.float32),
            jax.ShapeDtypeStruct(fwd_last.shape, jnp.float32),
        ),
        in_specs=[hbm, hbm, vmem, vmem, smem, smem, vmem, vmem, vmem],
        out_specs=(vmem, hbm),
        scratch_shapes=[
            even, even, odd, odd, odd, odd,
            pltpu.VMEM((2, HALO, wide, lanes), jnp.float32),
            pltpu.VMEM((wide // 8, depth, 8, lanes), jnp.float32),
            pltpu.VMEM((parts, n_x - 1, n_hi, depth // parts, 8, lanes), jnp.float32),
            pltpu.VMEM((parts, n_hi - 1, depth // parts, 8, lanes), jnp.float32),
            pltpu.VMEM((parts, n_hi, depth // parts, 8, lanes), jnp.float32),
            triple, triple, triple, triple,
            pltpu.SemaphoreType.DMA((2,)),
            pair, pair,
            pltpu.SemaphoreType.DMA((parts, n_x + n_hi - 2)),
            pltpu.SemaphoreType.DMA((parts, n_x + n_hi - 2)),
        ],
        compiler_params=pltpu.CompilerParams(
            collective_id=0, has_side_effects=True, vmem_limit_bytes=16 * 1024 * 1024
        ),
    )(fwd_last, fwd_prev, velocity, aperture, src_index, waves, table, mx, my)


def solution(mesh):
    in_specs = (
        P("shot", "slab", None, None),
        P("shot", "slab", None, None),
        P("slab", None, None),
        P("shot", None, None),
        P("shot", None),
        P("shot"),
        P("shot", None, None),
    )
    out_specs = (P("slab", "shot", None), P("shot", "slab", None, None))
    shots = mesh.shape["shot"]
    groups = (shots // 2, 2)
    return jax.shard_map(
        functools.partial(on_device, groups),
        mesh=mesh, in_specs=in_specs, out_specs=out_specs, check_vma=False,
    )
```

```python
import functools

import jax
import jax.numpy as jnp
import numpy as np
from jax import lax
from jax.experimental import pallas as pl
from jax.experimental.pallas import tpu as pltpu
from jax.sharding import PartitionSpec as P

SCALE = 5040.0
CENTRE = -43050.0
WEIGHTS = (8064.0, -1008.0, 128.0, -9.0)
HALO = 4
MESH = pl.DeviceIdType.MESH


def ricker(step):
    arg = (jnp.pi * 0.06 * (step - 10.0)) ** 2
    return 10.0 * (1.0 - 2.0 * arg) * jnp.exp(-arg)


def band(size):
    matrix = np.zeros((size, size), np.float32)
    for k, weight in enumerate(WEIGHTS, 1):
        matrix += weight * (np.eye(size, k=k) + np.eye(size, k=-k))
    return matrix


def table_kernel(first_row, rec_ref, res_ref, table, picked):
    steps, receivers = res_ref.shape[1:]
    lanes = table.shape[1]
    rows = table.shape[0] // steps
    base = (lax.axis_index("slab") * (rows - 2 * first_row) - first_row) * lanes
    lane_bits = lanes.bit_length() - 1
    group = 16
    clear_rows = rows * steps // (receivers // group)

    def scan(i, count):
        for j in range(group):
            r = i * group + j
            local = rec_ref[0, r] - base
            picked[count] = r
            inside = lax.shift_right_logical(local, lane_bits) < rows
            count = count + inside.astype(jnp.int32)
        clear = pl.multiple_of(i * clear_rows, clear_rows)
        table[pl.ds(clear, clear_rows)] = jnp.zeros((clear_rows, lanes), jnp.float32)
        return count

    count = lax.fori_loop(0, receivers // group, scan, jnp.int32(0))
    lane_ids = lax.broadcasted_iota(jnp.int32, (steps, lanes), 1)
    together = 4

    def add(i, carry):
        todo = []
        for j in range(together):
            index = i * together + j
            r = picked[jnp.minimum(index, count - 1)]
            local = rec_ref[0, r] - base
            row = lax.shift_right_logical(local, lane_bits)
            lane = local & (lanes - 1)
            start = pl.multiple_of(r - (r & (lanes - 1)), lanes)
            traces = res_ref[0, :, pl.ds(start, lanes)]
            moved = pltpu.roll(traces, (lane - r) & (lanes - 1), axis=1)
            chosen = jnp.where(index < count, lane, -1)
            todo.append((row, jnp.where(lane_ids == chosen, SCALE * moved, 0.0)))
        for row, value in todo:
            places = [pl.ds(row + n * rows, 8, stride=rows) for n in range(0, steps, 8)]
            held = [table[place, :] for place in places]
            for n, place in enumerate(places):
                table[place, :] = held[n] + value[8 * n : 8 * n + 8]
        return carry

    lax.fori_loop(0, (count + together - 1) // together, add, 0)


def receiver_table(rec_index, residual, depth, wide, lanes):
    steps = residual.shape[1]
    vmem = pl.BlockSpec(memory_space=pltpu.VMEM)
    rows = (depth + 2 * HALO) * wide
    return pl.pallas_call(
        functools.partial(table_kernel, HALO * wide),
        out_shape=jax.ShapeDtypeStruct((steps * rows, lanes), jnp.float32),
        in_specs=[pl.BlockSpec(memory_space=pltpu.SMEM), vmem],
        out_specs=vmem,
        scratch_shapes=[pltpu.SMEM((rec_index.shape[1],), jnp.int32)],
        compiler_params=pltpu.CompilerParams(vmem_limit_bytes=4 * 1024 * 1024),
        cost_estimate=pl.CostEstimate(flops=0, bytes_accessed=4 * steps * rows * lanes, transcendentals=0),
    )(rec_index, residual)


def adjoint_kernel(
    groups, last_ref, prev_ref, below_ref, above_ref, vel_ref, gate_ref, src_ref, wave_ref, rec_ref, mx_ref, my_ref,
    grad_ref, adj_ref,
    u_even, l_even, u_odd, l_odd, coef, src_coef, vel_halo, image, first, second, part_sum,
    u_send, u_recv, l_send, l_recv, io_sem, edge_sem, sum_send, sum_recv,
):
    depth, wide, lanes = last_ref.shape[1:]
    ring = 2 * HALO
    blocks = wave_ref.shape[0] // 2
    steps = 2 * blocks
    ext_rows = (depth + 2 * HALO) * wide
    n_x, n_hi = groups
    shot = lax.axis_index("shot")
    slab = lax.axis_index("slab")
    slabs = lax.axis_size("slab")
    x, hi = shot // n_hi, shot % n_hi
    has_down, has_up = slab > 0, slab < slabs - 1

    load_prev = pltpu.make_async_copy(prev_ref.at[0], u_even.at[0, pl.ds(ring, depth)], io_sem.at[0])
    load_last = pltpu.make_async_copy(last_ref.at[0], u_odd.at[pl.ds(HALO, depth)], io_sem.at[1])
    loads = [load_prev, load_last]
    for side, edge in ((0, below_ref), (1, above_ref)):
        for i, (first_layer, count, place) in enumerate((
            (0, ring, u_even.at[0, pl.ds(side * (depth + ring), ring)]),
            (ring, HALO, u_odd.at[pl.ds(side * (depth + HALO), HALO)]),
            (ring + HALO, HALO, vel_halo.at[side]),
        )):
            loads.append(
                pltpu.make_async_copy(edge.at[pl.ds(first_layer, count)], place, edge_sem.at[side, i])
            )
    for load in loads:
        load.start()

    empty = jnp.zeros((HALO, wide, lanes), jnp.float32)
    for z in range(0, depth + 2 * ring, HALO):
        l_even[0, z : z + HALO] = empty
        l_even[1, z : z + HALO] = empty
    for z in (0, HALO, depth + ring, depth + ring + HALO):
        u_even[1, z : z + HALO] = empty
    for z in range(0, depth + 2 * HALO, HALO):
        l_odd[z : z + HALO] = empty

    barrier = pltpu.get_barrier_semaphore()
    peers = [(lax.rem(x + d, n_x) * n_hi + hi, slab) for d in range(1, n_x)]
    peers += [(x * n_hi + lax.rem(hi + d, n_hi), slab) for d in range(1, n_hi)]
    for peer in peers:
        pl.semaphore_signal(barrier, inc=1, device_id=peer, device_id_type=MESH)

    @pl.when(has_down)
    def _():
        pl.semaphore_signal(barrier, inc=1, device_id=(shot, slab - 1), device_id_type=MESH)

    @pl.when(has_up)
    def _():
        pl.semaphore_signal(barrier, inc=1, device_id=(shot, slab + 1), device_id_type=MESH)

    pl.semaphore_wait(barrier, len(peers) + has_down.astype(jnp.int32) + has_up.astype(jnp.int32))

    def remote(src, dst, send, recv, target):
        return pltpu.make_async_remote_copy(
            src_ref=src, dst_ref=dst, send_sem=send, recv_sem=recv,
            device_id=target, device_id_type=MESH,
        )

    def halo_layers(side, half):
        return depth - HALO * (half + 1) if side else HALO * half

    def halo_copy(buf, send, recv, q, side, half):
        start = halo_layers(side, half)
        place = start - depth if side else start + depth
        return remote(
            buf.at[q, pl.ds(ring + start, HALO)], buf.at[q, pl.ds(ring + place, HALO)],
            send.at[q, side, half], recv.at[q, 1 - side, half], (shot, slab + (1 if side else -1)),
        )

    sides = ((0, has_down), (1, has_up))

    ids = lax.broadcasted_iota(jnp.int32, (wide, lanes), 0) * lanes + lax.broadcasted_iota(
        jnp.int32, (wide, lanes), 1
    )
    source = src_ref[0] - slab * (depth * wide * lanes)

    def prepare(z, speed):
        speed = 0.4 * speed
        value = speed * speed
        coef[z + HALO] = value * (1.0 / SCALE)
        src_coef[z + HALO] = jnp.where(ids == source - z * (wide * lanes), value, 0.0)

    def prepare_own(z, carry):
        prepare(z, vel_ref[z])
        image[:, z] = jnp.zeros((wide // 8, 8, lanes), jnp.float32)
        return carry

    lax.fori_loop(0, depth, prepare_own, 0)
    for load in loads:
        load.wait()
    for side in range(2):
        for z in range(HALO):
            prepare(z + (depth if side else -HALO), vel_halo[side, z])

    def laplace(read, z):
        f = read(z)
        hi_part = f.astype(jnp.bfloat16)
        rest = f - hi_part.astype(jnp.float32)
        mid_part = rest.astype(jnp.bfloat16)
        lo_part = (rest - mid_part.astype(jnp.float32)).astype(jnp.bfloat16)
        total = CENTRE * f
        for k, weight in enumerate(WEIGHTS, 1):
            total = total + weight * (read(z + k) + read(z - k))
        total = total + jnp.dot(
            mx_ref[...],
            jnp.concatenate([hi_part, mid_part, lo_part], axis=0),
            preferred_element_type=jnp.float32,
        )
        total = total + jnp.dot(
            jnp.concatenate([hi_part, mid_part, lo_part], axis=1),
            my_ref[...],
            preferred_element_type=jnp.float32,
        )
        return f, total

    def update(even, odd, q, to_odd, is_l, wave, rec_start, layers):
        read_even = lambda z: even[q, z + ring]
        read_odd = lambda z: odd[z + HALO]
        for z in layers:
            f, lap = laplace(read_even if to_odd else read_odd, z)
            earlier = (read_odd if to_odd else read_even)(z)
            place = z + HALO
            if is_l:
                start = pl.multiple_of(rec_start + place * wide, 8)
                lap = lap + rec_ref[pl.ds(start, wide), :]
                if 0 <= z < depth:
                    now = u_even[q, z + ring] if to_odd else u_odd[place]
                    image[:, z] = image[:, z] + (now * lap).reshape(wide // 8, 8, lanes)
                fresh = 2.0 * f - earlier + coef[place] * lap
            else:
                fresh = 2.0 * f - earlier + coef[place] * lap + wave * src_coef[place]
            if to_odd:
                odd[place] = fresh
            else:
                even[1 - q, z + ring] = fresh

    parts = 2
    rows = depth // parts

    def spread(c, d):
        target = lax.rem(x + d, n_x)
        return remote(
            image.at[pl.ds(target * n_hi, n_hi), pl.ds(c * rows, rows)], first.at[c, d - 1],
            sum_send.at[c, d - 1], sum_recv.at[c, d - 1], (target * n_hi + hi, slab),
        )

    def gather(c, d):
        target = lax.rem(hi + d, n_hi)
        return remote(
            part_sum.at[c, target], second.at[c, d - 1],
            sum_send.at[c, n_x - 2 + d], sum_recv.at[c, n_x - 2 + d], (x * n_hi + target, slab),
        )

    def spread_part(c):
        for p in range(wide // 8):
            gate = gate_ref[0, 8 * p : 8 * p + 8].astype(jnp.float32)
            image[p, c * rows : (c + 1) * rows] = image[p, c * rows : (c + 1) * rows] * gate
        for d in range(1, n_x):
            spread(c, d).start()

    assert depth == 4 * HALO
    fields = (
        (u_even, u_odd, u_send, u_recv, False),
        (l_even, l_odd, l_send, l_recv, True),
    )

    def layers(b, q, field, to_odd, some):
        even, odd, _, _, is_l = field
        i = 0 if to_odd else 1
        step = 2 * b + i
        rec_start = (steps - 1 - step) * ext_rows
        update(even, odd, q, to_odd, is_l, wave_ref[step], rec_start, some)

    def inner(b, q, field):
        layers(b, q, field, True, range(HALO, depth - HALO))

    def when(cond, run):
        if cond is True:
            run()
        else:
            pl.when(cond)(run)

    def both(a, b):
        return a if b is True else jnp.logical_and(a, b)

    def arrive(q, field, side, half, some):
        even, _, send, recv, _ = field
        when(both(sides[side][1], some), halo_copy(even, send, recv, q, 1 - side, half).wait_recv)

    def depart(b, q, field, side, half, sent_before, more):
        even, _, send, recv, _ = field
        has = sides[side][1]
        start = halo_layers(side, half)

        def second():
            when(both(has, sent_before), halo_copy(even, send, recv, 1 - q, side, half).wait_send)
            layers(b, q, field, False, range(start, start + HALO))

        if field[4]:
            second()
        else:
            when(more, second)
        when(both(has, more), halo_copy(even, send, recv, 1 - q, side, half).start)

    near_layers = (range(HALO), range(depth - HALO, depth))
    far_layers = (range(-HALO, 0), range(depth, depth + HALO))

    def near_first(i, field, side, half):
        b, q = 2 * i, 0
        arrive(q, field, side, half, i >= 1)
        layers(b, q, field, True, far_layers[side] if half else near_layers[side])
        depart(b, q, field, side, 1 - half, i >= 1, True)

    def far_first(i, field, side):
        b, q = 2 * i + 1, 1
        more = b < blocks - 1
        arrive(q, field, side, 1, True)
        arrive(q, field, side, 0, True)
        layers(b, q, field, True, near_layers[side])
        layers(b, q, field, True, far_layers[side])
        for half in range(2):
            depart(b, q, field, side, half, i >= 1, more)

    def two_blocks(i, carry):
        u, l = fields
        inner(2 * i, 0, u)
        near_first(i, u, 0, 0)
        near_first(i, u, 1, 0)
        inner(2 * i, 0, l)
        near_first(i, u, 0, 1)
        near_first(i, u, 1, 1)
        near_first(i, l, 0, 0)
        near_first(i, l, 1, 0)
        inner(2 * i + 1, 1, u)
        near_first(i, l, 0, 1)
        near_first(i, l, 1, 1)
        far_first(i, u, 0)
        far_first(i, u, 1)
        inner(2 * i + 1, 1, l)
        far_first(i, l, 0)

        @pl.when(i == blocks // 2 - 1)
        def _():
            spread_part(0)

        far_first(i, l, 1)
        return carry

    lax.fori_loop(0, blocks // 2, two_blocks, 0)
    spread_part(1)
    store = pltpu.make_async_copy(
        l_even.at[blocks % 2, pl.ds(ring, depth)], adj_ref.at[0], io_sem.at[0]
    )
    store.start()

    for c in range(parts):
        for d in range(1, n_x):
            spread(c, d).wait_recv()
        for h in range(n_hi):
            total = image[x * n_hi + h, c * rows : (c + 1) * rows]
            for d in range(1, n_x):
                total = total + first[c, d - 1, h]
            part_sum[c, h] = total
        for d in range(1, n_hi):
            gather(c, d).start()
    for c in range(parts):
        for d in range(1, n_hi):
            gather(c, d).wait_recv()
        total = part_sum[c, hi]
        for d in range(1, n_hi):
            total = total + second[c, d - 1]
        speed = vel_ref[pl.ds(c * rows, rows), pl.ds(pl.multiple_of(shot * 8, 8), 8), :]
        grad_ref[pl.ds(c * rows, rows)] = (-0.32 / SCALE) * speed * total
    for c in range(parts):
        for d in range(1, n_x):
            spread(c, d).wait_send()
        for d in range(1, n_hi):
            gather(c, d).wait_send()
    store.wait()

    for side, has in sides:
        @pl.when(has)
        def _():
            for half in range(2):
                halo_copy(u_even, u_send, u_recv, 0, side, half).wait_send()
                halo_copy(u_even, u_send, u_recv, 1, side, half).wait_send()
                halo_copy(l_even, l_send, l_recv, 1, side, half).wait_send()


def on_device(groups, fwd_last, fwd_prev, velocity, aperture, rec_index, src_index, residual):
    depth, wide, lanes = fwd_last.shape[1:]
    steps = residual.shape[1]
    n_x, n_hi = groups
    count = lax.axis_size("slab")
    upward = [(i, i + 1) for i in range(count - 1)]
    bottom = jnp.concatenate([fwd_prev[0, : 2 * HALO], fwd_last[0, :HALO], velocity[:HALO]])
    top = jnp.concatenate([fwd_prev[0, -2 * HALO :], fwd_last[0, -HALO:], velocity[-HALO:]])
    below = lax.ppermute(top, "slab", upward)
    above = lax.ppermute(bottom, "slab", [(j, i) for i, j in upward])
    table = receiver_table(rec_index, residual, depth, wide, lanes)
    waves = ricker((steps - 1 - jnp.arange(steps, dtype=jnp.int32)).astype(jnp.float32))
    mx = jnp.asarray(np.tile(band(wide), (1, 3)), jnp.bfloat16)
    my = jnp.asarray(np.tile(band(lanes), (3, 1)), jnp.bfloat16)
    hbm = pl.BlockSpec(memory_space=pl.ANY)
    vmem = pl.BlockSpec(memory_space=pltpu.VMEM)
    smem = pl.BlockSpec(memory_space=pltpu.SMEM)
    even = pltpu.VMEM((2, depth + 4 * HALO, wide, lanes), jnp.float32)
    odd = pltpu.VMEM((depth + 2 * HALO, wide, lanes), jnp.float32)
    triple = pltpu.SemaphoreType.DMA((2, 2, 2))
    parts = 2
    return pl.pallas_call(
        functools.partial(adjoint_kernel, groups),
        out_shape=(
            jax.ShapeDtypeStruct((depth, 8, lanes), jnp.float32),
            jax.ShapeDtypeStruct(fwd_last.shape, jnp.float32),
        ),
        in_specs=[hbm, hbm, hbm, hbm, vmem, vmem, smem, smem, vmem, vmem, vmem],
        out_specs=(vmem, hbm),
        scratch_shapes=[
            even, even, odd, odd, odd, odd,
            pltpu.VMEM((2, HALO, wide, lanes), jnp.float32),
            pltpu.VMEM((wide // 8, depth, 8, lanes), jnp.float32),
            pltpu.VMEM((parts, n_x - 1, n_hi, depth // parts, 8, lanes), jnp.float32),
            pltpu.VMEM((parts, n_hi - 1, depth // parts, 8, lanes), jnp.float32),
            pltpu.VMEM((parts, n_hi, depth // parts, 8, lanes), jnp.float32),
            triple, triple, triple, triple,
            pltpu.SemaphoreType.DMA((2,)),
            pltpu.SemaphoreType.DMA((2, 3)),
            pltpu.SemaphoreType.DMA((parts, n_x + n_hi - 2)),
            pltpu.SemaphoreType.DMA((parts, n_x + n_hi - 2)),
        ],
        compiler_params=pltpu.CompilerParams(
            collective_id=0, has_side_effects=True, vmem_limit_bytes=16 * 1024 * 1024
        ),
    )(fwd_last, fwd_prev, below, above, velocity, aperture, src_index, waves, table, mx, my)


def solution(mesh):
    in_specs = (
        P("shot", "slab", None, None),
        P("shot", "slab", None, None),
        P("slab", None, None),
        P("shot", None, None),
        P("shot", None),
        P("shot"),
        P("shot", None, None),
    )
    out_specs = (P("slab", "shot", None), P("shot", "slab", None, None))
    shots = mesh.shape["shot"]
    groups = (shots // 2, 2)
    return jax.shard_map(
        functools.partial(on_device, groups),
        mesh=mesh, in_specs=in_specs, out_specs=out_specs, check_vma=False,
    )
```

```python
import functools

import jax
import jax.numpy as jnp
import numpy as np
from jax import lax
from jax.experimental import pallas as pl
from jax.experimental.pallas import tpu as pltpu
from jax.sharding import PartitionSpec as P

SCALE = 5040.0
CENTRE = -43050.0
WEIGHTS = (8064.0, -1008.0, 128.0, -9.0)
HALO = 4
MESH = pl.DeviceIdType.MESH


def ricker(step):
    arg = (jnp.pi * 0.06 * (step - 10.0)) ** 2
    return 10.0 * (1.0 - 2.0 * arg) * jnp.exp(-arg)


def band(size):
    matrix = np.zeros((size, size), np.float32)
    for k, weight in enumerate(WEIGHTS, 1):
        matrix += weight * (np.eye(size, k=k) + np.eye(size, k=-k))
    return matrix


def table_kernel(first_row, rec_ref, res_ref, table, picked):
    steps, receivers = res_ref.shape[1:]
    lanes = table.shape[1]
    rows = table.shape[0] // steps
    base = (lax.axis_index("slab") * (rows - 2 * first_row) - first_row) * lanes
    lane_bits = lanes.bit_length() - 1
    group = 16
    clear_rows = rows * steps // (receivers // group)

    def scan(i, count):
        for j in range(group):
            r = i * group + j
            local = rec_ref[0, r] - base
            picked[count] = r
            inside = lax.shift_right_logical(local, lane_bits) < rows
            count = count + inside.astype(jnp.int32)
        clear = pl.multiple_of(i * clear_rows, clear_rows)
        table[pl.ds(clear, clear_rows)] = jnp.zeros((clear_rows, lanes), jnp.float32)
        return count

    count = lax.fori_loop(0, receivers // group, scan, jnp.int32(0))
    lane_ids = lax.broadcasted_iota(jnp.int32, (steps, lanes), 1)
    together = 4

    def add(i, carry):
        todo = []
        for j in range(together):
            index = i * together + j
            r = picked[jnp.minimum(index, count - 1)]
            local = rec_ref[0, r] - base
            row = lax.shift_right_logical(local, lane_bits)
            lane = local & (lanes - 1)
            start = pl.multiple_of(r - (r & (lanes - 1)), lanes)
            traces = res_ref[0, :, pl.ds(start, lanes)]
            moved = pltpu.roll(traces, (lane - r) & (lanes - 1), axis=1)
            chosen = jnp.where(index < count, lane, -1)
            todo.append((row, jnp.where(lane_ids == chosen, SCALE * moved, 0.0)))
        for row, value in todo:
            places = [pl.ds(row + n * rows, 8, stride=rows) for n in range(0, steps, 8)]
            held = [table[place, :] for place in places]
            for n, place in enumerate(places):
                table[place, :] = held[n] + value[8 * n : 8 * n + 8]
        return carry

    lax.fori_loop(0, (count + together - 1) // together, add, 0)


def receiver_table(rec_index, residual, depth, wide, lanes):
    steps = residual.shape[1]
    vmem = pl.BlockSpec(memory_space=pltpu.VMEM)
    rows = (depth + 2 * HALO) * wide
    return pl.pallas_call(
        functools.partial(table_kernel, HALO * wide),
        out_shape=jax.ShapeDtypeStruct((steps * rows, lanes), jnp.float32),
        in_specs=[pl.BlockSpec(memory_space=pltpu.SMEM), vmem],
        out_specs=vmem,
        scratch_shapes=[pltpu.SMEM((rec_index.shape[1],), jnp.int32)],
        compiler_params=pltpu.CompilerParams(vmem_limit_bytes=4 * 1024 * 1024),
        cost_estimate=pl.CostEstimate(flops=0, bytes_accessed=4 * steps * rows * lanes, transcendentals=0),
    )(rec_index, residual)


def adjoint_kernel(
    groups, last_ref, prev_ref, vel_ref, gate_ref, src_ref, wave_ref, rec_ref, mx_ref, my_ref,
    grad_ref, adj_ref,
    u_even, l_even, u_odd, l_odd, coef, src_coef, vel_halo, image, first, second, part_sum,
    u_send, u_recv, l_send, l_recv, io_sem, start_send, start_recv, sum_send, sum_recv,
):
    depth, wide, lanes = last_ref.shape[1:]
    ring = 2 * HALO
    blocks = wave_ref.shape[0] // 2
    steps = 2 * blocks
    ext_rows = (depth + 2 * HALO) * wide
    n_x, n_hi = groups
    shot = lax.axis_index("shot")
    slab = lax.axis_index("slab")
    slabs = lax.axis_size("slab")
    x, hi = shot // n_hi, shot % n_hi
    has_down, has_up = slab > 0, slab < slabs - 1

    load_prev = pltpu.make_async_copy(prev_ref.at[0], u_even.at[0, pl.ds(ring, depth)], io_sem.at[0])
    load_last = pltpu.make_async_copy(last_ref.at[0], u_odd.at[pl.ds(HALO, depth)], io_sem.at[1])
    load_prev.start()
    load_last.start()

    empty = jnp.zeros((HALO, wide, lanes), jnp.float32)
    for z in range(0, depth + 2 * ring, HALO):
        l_even[0, z : z + HALO] = empty
        l_even[1, z : z + HALO] = empty
    for z in (0, HALO, depth + ring, depth + ring + HALO):
        u_even[0, z : z + HALO] = empty
        u_even[1, z : z + HALO] = empty
    for z in range(0, depth + 2 * HALO, HALO):
        l_odd[z : z + HALO] = empty
    for side, z in ((0, 0), (1, depth + HALO)):
        u_odd[z : z + HALO] = empty
        vel_halo[side] = empty

    barrier = pltpu.get_barrier_semaphore()
    peers = [(lax.rem(x + d, n_x) * n_hi + hi, slab) for d in range(1, n_x)]
    peers += [(x * n_hi + lax.rem(hi + d, n_hi), slab) for d in range(1, n_hi)]
    for peer in peers:
        pl.semaphore_signal(barrier, inc=1, device_id=peer, device_id_type=MESH)

    @pl.when(has_down)
    def _():
        pl.semaphore_signal(barrier, inc=1, device_id=(shot, slab - 1), device_id_type=MESH)

    @pl.when(has_up)
    def _():
        pl.semaphore_signal(barrier, inc=1, device_id=(shot, slab + 1), device_id_type=MESH)

    pl.semaphore_wait(barrier, len(peers) + has_down.astype(jnp.int32) + has_up.astype(jnp.int32))

    def remote(src, dst, send, recv, target):
        return pltpu.make_async_remote_copy(
            src_ref=src, dst_ref=dst, send_sem=send, recv_sem=recv,
            device_id=target, device_id_type=MESH,
        )

    def halo_layers(side, half):
        return depth - HALO * (half + 1) if side else HALO * half

    def halo_copy(buf, send, recv, q, side, half, source=None):
        start = halo_layers(side, half)
        place = start - depth if side else start + depth
        src = buf.at[q, pl.ds(ring + start, HALO)] if source is None else source
        return remote(
            src, buf.at[q, pl.ds(ring + place, HALO)],
            send.at[q, side, half], recv.at[q, 1 - side, half], (shot, slab + (1 if side else -1)),
        )

    def start_copies(side):
        near = pl.ds(halo_layers(side, 0), HALO)
        far = pl.ds(halo_layers(side, 1), HALO)
        odd_place = pl.ds(0, HALO) if side else pl.ds(depth + HALO, HALO)
        target = (shot, slab + (1 if side else -1))
        return (
            remote(
                vel_ref.at[near], vel_halo.at[1 - side],
                start_send.at[0, side], start_recv.at[0, 1 - side], target,
            ),
            halo_copy(u_even, u_send, u_recv, 0, side, 0, prev_ref.at[0, near]),
            halo_copy(u_even, u_send, u_recv, 0, side, 1, prev_ref.at[0, far]),
            remote(
                last_ref.at[0, near], u_odd.at[odd_place],
                start_send.at[1, side], start_recv.at[1, 1 - side], target,
            ),
        )

    sides = ((0, has_down), (1, has_up))
    for side, has in sides:
        @pl.when(has)
        def _():
            velocity_out, near_out, far_out, last_out = start_copies(side)
            for copy in (near_out, far_out, last_out, velocity_out):
                copy.start()

    ids = lax.broadcasted_iota(jnp.int32, (wide, lanes), 0) * lanes + lax.broadcasted_iota(
        jnp.int32, (wide, lanes), 1
    )
    source = src_ref[0] - slab * (depth * wide * lanes)

    def prepare(z, speed):
        speed = 0.4 * speed
        value = speed * speed
        coef[z + HALO] = value * (1.0 / SCALE)
        src_coef[z + HALO] = jnp.where(ids == source - z * (wide * lanes), value, 0.0)

    def prepare_own(z, carry):
        prepare(z, vel_ref[z])
        image[:, z] = jnp.zeros((wide // 8, 8, lanes), jnp.float32)
        return carry

    lax.fori_loop(0, depth, prepare_own, 0)
    load_prev.wait()
    load_last.wait()
    def first_halo():
        for side, has in sides:
            @pl.when(has)
            def _():
                velocity_in, _, _, last_in = start_copies(1 - side)
                last_in.wait_recv()
                velocity_in.wait_recv()

            for z in range(HALO):
                prepare(z + (depth if side else -HALO), vel_halo[side, z])

    def laplace(read, z):
        f = read(z)
        hi_part = f.astype(jnp.bfloat16)
        rest = f - hi_part.astype(jnp.float32)
        mid_part = rest.astype(jnp.bfloat16)
        lo_part = (rest - mid_part.astype(jnp.float32)).astype(jnp.bfloat16)
        total = CENTRE * f
        for k, weight in enumerate(WEIGHTS, 1):
            total = total + weight * (read(z + k) + read(z - k))
        total = total + jnp.dot(
            mx_ref[...],
            jnp.concatenate([hi_part, mid_part, lo_part], axis=0),
            preferred_element_type=jnp.float32,
        )
        total = total + jnp.dot(
            jnp.concatenate([hi_part, mid_part, lo_part], axis=1),
            my_ref[...],
            preferred_element_type=jnp.float32,
        )
        return f, total

    def update(even, odd, q, to_odd, is_l, wave, rec_start, layers):
        read_even = lambda z: even[q, z + ring]
        read_odd = lambda z: odd[z + HALO]
        for z in layers:
            f, lap = laplace(read_even if to_odd else read_odd, z)
            earlier = (read_odd if to_odd else read_even)(z)
            place = z + HALO
            if is_l:
                start = pl.multiple_of(rec_start + place * wide, 8)
                lap = lap + rec_ref[pl.ds(start, wide), :]
                if 0 <= z < depth:
                    now = u_even[q, z + ring] if to_odd else u_odd[place]
                    image[:, z] = image[:, z] + (now * lap).reshape(wide // 8, 8, lanes)
                fresh = 2.0 * f - earlier + coef[place] * lap
            else:
                fresh = 2.0 * f - earlier + coef[place] * lap + wave * src_coef[place]
            if to_odd:
                odd[place] = fresh
            else:
                even[1 - q, z + ring] = fresh

    parts = 2
    rows = depth // parts

    def spread(c, d):
        target = lax.rem(x + d, n_x)
        return remote(
            image.at[pl.ds(target * n_hi, n_hi), pl.ds(c * rows, rows)], first.at[c, d - 1],
            sum_send.at[c, d - 1], sum_recv.at[c, d - 1], (target * n_hi + hi, slab),
        )

    def gather(c, d):
        target = lax.rem(hi + d, n_hi)
        return remote(
            part_sum.at[c, target], second.at[c, d - 1],
            sum_send.at[c, n_x - 2 + d], sum_recv.at[c, n_x - 2 + d], (x * n_hi + target, slab),
        )

    def spread_part(c):
        for p in range(wide // 8):
            gate = gate_ref[0, 8 * p : 8 * p + 8].astype(jnp.float32)
            image[p, c * rows : (c + 1) * rows] = image[p, c * rows : (c + 1) * rows] * gate
        for d in range(1, n_x):
            spread(c, d).start()

    assert depth == 4 * HALO
    fields = (
        (u_even, u_odd, u_send, u_recv, False),
        (l_even, l_odd, l_send, l_recv, True),
    )

    def layers(b, q, field, to_odd, some):
        even, odd, _, _, is_l = field
        i = 0 if to_odd else 1
        step = 2 * b + i
        rec_start = (steps - 1 - step) * ext_rows
        update(even, odd, q, to_odd, is_l, wave_ref[step], rec_start, some)

    def inner(b, q, field):
        layers(b, q, field, True, range(HALO, depth - HALO))

    def when(cond, run):
        if cond is True:
            run()
        else:
            pl.when(cond)(run)

    def both(a, b):
        return a if b is True else jnp.logical_and(a, b)

    def arrive(q, field, side, half, some):
        even, _, send, recv, _ = field
        when(both(sides[side][1], some), halo_copy(even, send, recv, q, 1 - side, half).wait_recv)

    def depart(b, q, field, side, half, sent_before, more):
        even, _, send, recv, _ = field
        has = sides[side][1]
        start = halo_layers(side, half)

        def second():
            when(both(has, sent_before), halo_copy(even, send, recv, 1 - q, side, half).wait_send)
            layers(b, q, field, False, range(start, start + HALO))

        if field[4]:
            second()
        else:
            when(more, second)
        when(both(has, more), halo_copy(even, send, recv, 1 - q, side, half).start)

    near_layers = (range(HALO), range(depth - HALO, depth))
    far_layers = (range(-HALO, 0), range(depth, depth + HALO))

    def near_first(i, field, side, half):
        b, q = 2 * i, 0
        arrive(q, field, side, half, i >= 1 if field[4] else True)
        layers(b, q, field, True, far_layers[side] if half else near_layers[side])
        depart(b, q, field, side, 1 - half, i >= 1, True)

    def far_first(i, field, side):
        b, q = 2 * i + 1, 1
        more = b < blocks - 1
        arrive(q, field, side, 1, True)
        arrive(q, field, side, 0, True)
        layers(b, q, field, True, near_layers[side])
        layers(b, q, field, True, far_layers[side])
        for half in range(2):
            depart(b, q, field, side, half, i >= 1 if field[4] else True, more)

    def two_blocks(i, carry):
        u, l = fields
        inner(2 * i, 0, u)
        near_first(i, u, 0, 0)
        near_first(i, u, 1, 0)
        inner(2 * i, 0, l)
        pl.when(i == 0)(first_halo)
        near_first(i, u, 0, 1)
        near_first(i, u, 1, 1)
        near_first(i, l, 0, 0)
        near_first(i, l, 1, 0)
        inner(2 * i + 1, 1, u)
        near_first(i, l, 0, 1)
        near_first(i, l, 1, 1)
        far_first(i, u, 0)
        far_first(i, u, 1)
        inner(2 * i + 1, 1, l)
        far_first(i, l, 0)

        @pl.when(i == blocks // 2 - 1)
        def _():
            spread_part(0)

        far_first(i, l, 1)
        return carry

    lax.fori_loop(0, blocks // 2, two_blocks, 0)
    spread_part(1)
    store = pltpu.make_async_copy(
        l_even.at[blocks % 2, pl.ds(ring, depth)], adj_ref.at[0], io_sem.at[0]
    )
    store.start()

    for c in range(parts):
        for d in range(1, n_x):
            spread(c, d).wait_recv()
        for h in range(n_hi):
            total = image[x * n_hi + h, c * rows : (c + 1) * rows]
            for d in range(1, n_x):
                total = total + first[c, d - 1, h]
            part_sum[c, h] = total
        for d in range(1, n_hi):
            gather(c, d).start()
    for c in range(parts):
        for d in range(1, n_hi):
            gather(c, d).wait_recv()
        total = part_sum[c, hi]
        for d in range(1, n_hi):
            total = total + second[c, d - 1]
        speed = vel_ref[pl.ds(c * rows, rows), pl.ds(pl.multiple_of(shot * 8, 8), 8), :]
        grad_ref[pl.ds(c * rows, rows)] = (-0.32 / SCALE) * speed * total
    for c in range(parts):
        for d in range(1, n_x):
            spread(c, d).wait_send()
        for d in range(1, n_hi):
            gather(c, d).wait_send()
    store.wait()

    for side, has in sides:
        @pl.when(has)
        def _():
            velocity_out, _, _, last_out = start_copies(side)
            velocity_out.wait_send()
            last_out.wait_send()
            for half in range(2):
                halo_copy(u_even, u_send, u_recv, 0, side, half).wait_send()
                halo_copy(u_even, u_send, u_recv, 1, side, half).wait_send()
                halo_copy(l_even, l_send, l_recv, 1, side, half).wait_send()


def on_device(groups, fwd_last, fwd_prev, velocity, aperture, rec_index, src_index, residual):
    depth, wide, lanes = fwd_last.shape[1:]
    steps = residual.shape[1]
    n_x, n_hi = groups
    table = receiver_table(rec_index, residual, depth, wide, lanes)
    waves = ricker((steps - 1 - jnp.arange(steps, dtype=jnp.int32)).astype(jnp.float32))
    mx = jnp.asarray(np.tile(band(wide), (1, 3)), jnp.bfloat16)
    my = jnp.asarray(np.tile(band(lanes), (3, 1)), jnp.bfloat16)
    hbm = pl.BlockSpec(memory_space=pl.ANY)
    vmem = pl.BlockSpec(memory_space=pltpu.VMEM)
    smem = pl.BlockSpec(memory_space=pltpu.SMEM)
    even = pltpu.VMEM((2, depth + 4 * HALO, wide, lanes), jnp.float32)
    odd = pltpu.VMEM((depth + 2 * HALO, wide, lanes), jnp.float32)
    pair = pltpu.SemaphoreType.DMA((2, 2))
    triple = pltpu.SemaphoreType.DMA((2, 2, 2))
    parts = 2
    return pl.pallas_call(
        functools.partial(adjoint_kernel, groups),
        out_shape=(
            jax.ShapeDtypeStruct((depth, 8, lanes), jnp.float32),
            jax.ShapeDtypeStruct(fwd_last.shape, jnp.float32),
        ),
        in_specs=[hbm, hbm, vmem, vmem, smem, smem, vmem, vmem, vmem],
        out_specs=(vmem, hbm),
        scratch_shapes=[
            even, even, odd, odd, odd, odd,
            pltpu.VMEM((2, HALO, wide, lanes), jnp.float32),
            pltpu.VMEM((wide // 8, depth, 8, lanes), jnp.float32),
            pltpu.VMEM((parts, n_x - 1, n_hi, depth // parts, 8, lanes), jnp.float32),
            pltpu.VMEM((parts, n_hi - 1, depth // parts, 8, lanes), jnp.float32),
            pltpu.VMEM((parts, n_hi, depth // parts, 8, lanes), jnp.float32),
            triple, triple, triple, triple,
            pltpu.SemaphoreType.DMA((2,)),
            pair, pair,
            pltpu.SemaphoreType.DMA((parts, n_x + n_hi - 2)),
            pltpu.SemaphoreType.DMA((parts, n_x + n_hi - 2)),
        ],
        compiler_params=pltpu.CompilerParams(
            collective_id=0, has_side_effects=True, vmem_limit_bytes=16 * 1024 * 1024
        ),
    )(fwd_last, fwd_prev, velocity, aperture, src_index, waves, table, mx, my)


def solution(mesh):
    in_specs = (
        P("shot", "slab", None, None),
        P("shot", "slab", None, None),
        P("slab", None, None),
        P("shot", None, None),
        P("shot", None),
        P("shot"),
        P("shot", None, None),
    )
    out_specs = (P("slab", "shot", None), P("shot", "slab", None, None))
    shots = mesh.shape["shot"]
    groups = (shots // 2, 2)
    return jax.shard_map(
        functools.partial(on_device, groups),
        mesh=mesh, in_specs=in_specs, out_specs=out_specs, check_vma=False,
    )
```
